32 devices in a mesh: groups: 2 (over y), tensor: 16 (over z, x, core).
Axes of the slice: x: 2, y: 2, z: 4, core: 2. Of those that a mesh axis runs over, the one named last changes fastest.
Arguments:
- grad_out: bfloat16 [64, 8192], P(('groups', 'tensor')), parts along dimension 0, may hold values from -6 to 6
- hidden: bfloat16 [64, 28672], P('groups', 'tensor'), parts along dimension 0, may hold values from -1 to 1
- down_weight: bfloat16 [28672, 8192], P('tensor'), may hold values from -0.03125 to 0.03125
- proj_in: bfloat16 [28672, 64], P('tensor'), may hold values from -0.1875 to 0.1875
- proj_out: bfloat16 [8192, 64], replicated, may hold values from -0.0625 to 0.0625
- example_lengths: int32 [32], P('groups'), parts along dimension 0, may hold values from 1 to 8, 32 in all
- owner_counts: int32 [32], P('groups'), parts along dimension 0, may hold values from 0 to 3, as said below
Outputs:
- grad_weight: bfloat16 [57344, 8192], P(('groups', 'tensor')), parts along dimension 0
- grad_hidden: bfloat16 [64, 28672], P('groups', 'tensor'), parts along dimension 0
- sketches: float32 [96, 4096], P(('groups', 'tensor')), parts along dimension 0
The draws below stay inside these ranges and needn't reach their ends.
There are 2 independent parts, one for each index of `groups`. The reference program is written for one: setup_inputs(seed, part) draws one part's arguments, and reference() takes and returns one part's arrays. A program takes and returns all parts, laid end to end along the dimension named above; an argument that names none is the same for every part. Nothing has to cross between parts.
Inputs may be any that keep to these rules, and one draw needn't show every extreme that they name: Example e covers the next example_lengths[e] tokens after the examples before it; the lengths sum to 32; some example has exactly 8 tokens. `owner_counts`: owner o owns the examples that begin at the sum of the counts of the owners before it, in order; the counts sum to 16; some owner holds exactly 3.
All inputs are finite; a program needn't handle non-finite values.
Results may differ from the reference program's by a relative error of at most 0.001.
Values may be sent and summed in bfloat16 or wider, within the bound.
A program may use at most 128 MiB of HBM per device.

```python
import math
import jax
import jax.numpy as jnp
import numpy as np
from jax import lax

D = 8192
FF = 28672
RANK = 64
OWN_CAP = 3
TOKENS = 32
EXAMPLES = 16
LEN_MAX = 8
N_TENSOR = 16


def draw_owner_counts(key, part):
    key = jax.random.fold_in(key, 7)
    perm_key, many_key = jax.random.split(key)
    order_ids = jax.random.permutation(perm_key, N_TENSOR)
    heavy_owners = jax.random.randint(many_key, (), 1, N_TENSOR // (2 * OWN_CAP) + 1)
    counts = jnp.where(order_ids < heavy_owners, OWN_CAP, jnp.where(order_ids < heavy_owners * OWN_CAP, 0, 1))
    return counts.astype(jnp.int32)


def steps_of(rng, shape, pieces, low, high):
    factor_of = 1.0
    for position, parts in pieces:
        steps = jax.random.uniform(jax.random.fold_in(jax.random.fold_in(rng, 6), position), (parts,), jnp.float32, low / len(pieces), high / len(pieces))
        factor_of = factor_of * jnp.repeat(jnp.exp(steps), shape[position] // parts).reshape((-1,) + (1,) * (len(shape) - 1 - position))
    return factor_of


def split_up(amount, total, bound, lean):
    loads = [(1 << 20) // math.isqrt(grade ** lean) + 1 for grade in range(2, amount + 1)]
    spare, given = total - bound - (amount - 1), [1] * (amount - 1)
    while spare > 0:
        candidates = [i for i in range(amount - 1) if given[i] < bound]
        whole, remaining = sum([loads[i] for i in candidates]), spare
        for i in candidates:
            more = min(bound - given[i], max(1, remaining * loads[i] // whole), spare)
            given[i] = given[i] + more
            spare = spare - more
    return np.array([bound] + given)


def ragged(stream_key, amount, total, reach, lean):
    if amount == 2:
        one = jax.random.randint(stream_key, (), max(1, total - reach), min(reach, total - 1) + 1)
        return jnp.stack([one, total - one])
    tallies = jnp.asarray(split_up(amount, total, reach, lean), jnp.int32)
    pairs = (amount - 1) // 2
    source_of, sink = tallies[1:1 + 2 * pairs:2], tallies[2:2 + 2 * pairs:2]
    margin = jnp.minimum(source_of - 1, reach - sink)
    shifted = jax.random.randint(jax.random.fold_in(stream_key, 1), (pairs,), 0, 1 << 20) % (margin + 1)
    tallies = tallies.at[1:1 + 2 * pairs:2].set(source_of - shifted).at[2:2 + 2 * pairs:2].set(sink + shifted)
    return tallies[jax.random.permutation(jax.random.fold_in(stream_key, 2), amount)]


def noise(key, shape, width, bound, cuts=(), kind=jnp.bfloat16):
    array = jax.random.normal(key, shape, jnp.float32) * width
    if len(cuts) > 0:
        array = steps_of(key, shape, cuts, -0.22, 0.18) * array
    return jnp.clip(array, min=-bound, max=bound).astype(kind)


def setup_inputs(seed: int = 0, part: int = 0) -> dict:
    streams_of = jax.random.split(jax.random.key(seed), 8)
    own_keys = jax.random.split(jax.random.fold_in(streams_of[7], part), 8)
    grad_out = noise(own_keys[0], (TOKENS, D), 1.0, 6.0, ((0, 16),))
    hidden = noise(own_keys[1], (TOKENS, FF), TOKENS ** -0.5, 1.0, ((1, 16),))
    down_weight = noise(streams_of[2], (FF, D), FF ** -0.5, 0.03125, ((0, 16),))
    proj_in = noise(streams_of[3], (FF, RANK), (max(FF // TOKENS, 1)) ** -0.5, 0.1875, ((0, 16),))
    proj_out = noise(streams_of[4], (D, RANK), D ** -0.5, 0.0625)
    example_lengths = ragged(own_keys[5], EXAMPLES, TOKENS, LEN_MAX, 2).astype(jnp.int32)
    owner_counts = draw_owner_counts(jax.random.fold_in(jax.random.fold_in(streams_of[7], part), 71), part)
    return {"grad_out": grad_out, "hidden": hidden, "down_weight": down_weight, "proj_in": proj_in, "proj_out": proj_out, "example_lengths": example_lengths, "owner_counts": owner_counts}


def table_lookup(table, index):
    hits = index[:, None] == jnp.arange(table.shape[0], dtype=jnp.int32)[None, :]
    return jnp.sum(jnp.where(hits, table[None, :], 0), axis=1).astype(jnp.int32)


def slot_members(example_lengths, owner_counts, token_total, slot_cap):
    example_start = (jnp.cumsum(example_lengths) - example_lengths).astype(jnp.int32)
    owner_first = (jnp.cumsum(owner_counts) - owner_counts).astype(jnp.int32)
    slot_ids = jnp.arange(owner_counts.shape[0] * slot_cap, dtype=jnp.int32)
    slot_owner = slot_ids // slot_cap
    slot_place = slot_ids % slot_cap
    slot_live = slot_place < table_lookup(owner_counts, slot_owner)
    example_id = table_lookup(owner_first, slot_owner) + slot_place
    begin_token = table_lookup(example_start, example_id)
    end_token = begin_token + table_lookup(example_lengths, example_id)
    positions = jnp.arange(token_total, dtype=jnp.int32)
    inside = (positions[None, :] >= begin_token[:, None]) & (positions[None, :] < end_token[:, None])
    return (inside & slot_live[:, None]).astype(jnp.float32)


def reference(grad_out, hidden, down_weight, proj_in, proj_out, example_lengths, owner_counts):
    grad_hidden = jnp.dot(grad_out, down_weight.T, preferred_element_type=jnp.float32).astype(jnp.bfloat16)
    grad_weight = jnp.dot(hidden.T, grad_out, preferred_element_type=jnp.float32).astype(jnp.bfloat16)
    hidden_proj = jnp.dot(hidden, proj_in, preferred_element_type=jnp.float32)
    grad_proj = jnp.dot(grad_out, proj_out, preferred_element_type=jnp.float32)
    member = slot_members(example_lengths, owner_counts, TOKENS, OWN_CAP)
    kron_terms = (hidden_proj[:, :, None] * grad_proj[:, None, :]).reshape(TOKENS, RANK * RANK)
    sketches = jnp.dot(member, kron_terms, precision=lax.Precision.HIGHEST, preferred_element_type=jnp.float32)
    return grad_weight, grad_hidden, sketches
```

```python
import functools
import jax
import jax.numpy as jnp
from jax import lax
from jax.experimental import pallas as pl
from jax.experimental.pallas import tpu as pltpu
from jax.sharding import PartitionSpec as P

OWN_CAP = 3
SLOW = 4
NT = (((1,), (1,)), ((), ()))
TN = (((0,), (0,)), ((), ()))
F32 = jnp.float32
BF16 = jnp.bfloat16


def row_tile(width):
    return 256 if width % 256 == 0 else width


def gather_kernel(
    fast, g_ref, hid_ref, pin_ref, w_ref, all_ref, gh_ref, hp_ref,
    buf, wide, wbuf, part, stage_a, stage_b, stage_c, wsem,
    s1s, s1r, s2s, s2r, s3s, s3r, pas, par, pbs, pbr, pcs, pcr,
):
    me = lax.axis_index("tensor")
    core = lax.rem(me, 2)
    chip = lax.div(me, 2)
    b = lax.rem(chip, fast)
    a = lax.div(chip, fast)
    blocks = buf.shape[0]
    rows = wbuf.shape[0]
    tile = row_tile(rows)
    tiles = rows // tile

    for i in range(tiles):
        pltpu.make_async_copy(
            w_ref.at[pl.ds(i * tile, tile)], wbuf.at[pl.ds(i * tile, tile)], wsem.at[i]
        ).start()

    def index(ai, bi, ci):
        return (ai * fast + bi) * 2 + ci

    def up(value, step, size):
        return lax.rem(value + step, size)

    def down(value, step, size):
        return lax.rem(value + size - step, size)

    barrier = pltpu.get_barrier_semaphore()
    peers = [index(up(a, s, SLOW), b, core) for s in range(1, SLOW)]
    peers += [index(a, up(b, r, fast), core) for r in range(1, fast)]
    peers += [index(a, b, 1 - core)]
    for peer in peers:
        pl.semaphore_signal(barrier, inc=1, device_id={"tensor": peer}, device_id_type=pl.DeviceIdType.MESH)
    buf[me] = g_ref[...]
    part[0] = lax.dot_general(hid_ref[...], pin_ref[...], NT, preferred_element_type=F32)
    pl.semaphore_wait(barrier, len(peers))

    def send(src, dst, ssem, rsem, peer):
        return pltpu.make_async_remote_copy(
            src_ref=src, dst_ref=dst, send_sem=ssem, recv_sem=rsem,
            device_id={"tensor": peer}, device_id_type=pl.DeviceIdType.MESH,
        )

    sends = []

    def go(copy):
        copy.start()
        sends.append(copy)

    def block(i):
        return buf.at[i]

    def to_sibling(s, r):
        i = index(down(a, s, SLOW), down(b, r, fast), core)
        go(send(block(i), block(i), s3s.at[s, r], s3r.at[s, r], index(a, b, 1 - core)))

    def to_fast(s):
        i = index(down(a, s, SLOW), b, core)
        for r in range(1, fast):
            go(send(block(i), block(i), s2s.at[s, r], s2r.at[s, r], index(a, up(b, r, fast), core)))
        to_sibling(s, 0)

    def landed(s, r, c, sem):
        i = index(down(a, s, SLOW), down(b, r, fast), c)
        send(block(i), block(i), sem, sem, index(a, b, 1 - core)).wait_recv()

    for s in (2, 1, 3):
        go(send(block(me), block(me), s1s.at[s], s1r.at[s], index(up(a, s, SLOW), b, core)))
    to_fast(0)
    for s in range(1, SLOW):
        go(send(part.at[0], stage_a.at[s], pas.at[s], par.at[s], index(up(a, s, SLOW), b, core)))
    for s in (1, 3, 2):
        landed(s, 0, core, s1r.at[s])
        to_fast(s)
    total = part[0]
    for s in range(1, SLOW):
        send(stage_a.at[s], stage_a.at[s], par.at[s], par.at[s], index(a, b, 1 - core)).wait_recv()
        total = total + stage_a[s]
    part[1] = total
    for r in range(1, fast):
        go(send(part.at[1], stage_b.at[r], pbs.at[r], pbr.at[r], index(a, up(b, r, fast), core)))
    for s in (0, 1, 3, 2):
        for r in range(1, fast):
            landed(s, r, core, s2r.at[s, r])
            to_sibling(s, r)
    for r in range(1, fast):
        send(stage_b.at[r], stage_b.at[r], pbr.at[r], pbr.at[r], index(a, b, 1 - core)).wait_recv()
        total = total + stage_b[r]
    part[2] = total
    go(send(part.at[2], stage_c.at[0], pcs.at[0], pcr.at[0], index(a, b, 1 - core)))
    for s in (0, 1, 3, 2):
        for r in range(fast):
            landed(s, r, 1 - core, s3r.at[s, r])

    width = buf.shape[2]
    per = buf.shape[1]
    for d in range(blocks):
        wide[d * per : (d + 1) * per, :] = buf[d].astype(F32)
    all_ref[...] = wide[...].astype(BF16)

    for i in range(tiles):
        pltpu.make_async_copy(
            w_ref.at[pl.ds(i * tile, tile)], wbuf.at[pl.ds(i * tile, tile)], wsem.at[i]
        ).wait()
        gh_ref[:, i * tile : (i + 1) * tile] = lax.dot_general(
            all_ref[...], wbuf[i * tile : (i + 1) * tile, :], NT, preferred_element_type=F32
        ).astype(BF16)

    send(stage_c.at[0], stage_c.at[0], pcr.at[0], pcr.at[0], index(a, b, 1 - core)).wait_recv()
    hp_ref[...] = total + stage_c[0]
    for copy in sends:
        copy.wait_send()


def gather(tensor, g, hidden, pin_t, w):
    per, width = g.shape
    tokens, rows = hidden.shape
    rank = pin_t.shape[0]
    fast = tensor // (2 * SLOW)
    dma = pltpu.SemaphoreType.DMA
    vmem = pl.BlockSpec(memory_space=pltpu.VMEM)
    return pl.pallas_call(
        functools.partial(gather_kernel, fast),
        out_shape=(
            jax.ShapeDtypeStruct((tokens, width), BF16),
            jax.ShapeDtypeStruct((tokens, rows), BF16),
            jax.ShapeDtypeStruct((tokens, rank), F32),
        ),
        in_specs=[vmem, vmem, vmem, pl.BlockSpec(memory_space=pl.ANY)],
        out_specs=(vmem, vmem, vmem),
        scratch_shapes=[
            pltpu.VMEM((tensor, per, width), BF16),
            pltpu.VMEM((tokens, width), F32),
            pltpu.VMEM((rows, width), BF16),
            pltpu.VMEM((3, tokens, rank), F32),
            pltpu.VMEM((SLOW, tokens, rank), F32),
            pltpu.VMEM((fast, tokens, rank), F32),
            pltpu.VMEM((1, tokens, rank), F32),
            dma((rows // row_tile(rows),)),
            dma((SLOW,)), dma((SLOW,)),
            dma((SLOW, fast)), dma((SLOW, fast)),
            dma((SLOW, fast)), dma((SLOW, fast)),
            dma((SLOW,)), dma((SLOW,)),
            dma((fast,)), dma((fast,)),
            dma((1,)), dma((1,)),
        ],
        compiler_params=pltpu.CompilerParams(
            collective_id=0, has_side_effects=True, vmem_limit_bytes=58 * 2**20
        ),
        name="gather_and_grad_hidden",
    )(g, hidden, pin_t, w)


def weight_kernel(
    len_ref, cnt_ref, me_ref, hid_ref, all_ref, gh_in, hp_ref, pout_ref,
    gw_ref, gh_ref, sk_ref,
):
    gw_ref[...] = lax.dot_general(
        hid_ref[...], all_ref[...], TN, preferred_element_type=F32
    ).astype(BF16)

    @pl.when(pl.program_id(0) == 1 % pl.num_programs(0))
    def _():
        gh_ref[...] = gh_in[...]
        tokens, rank = hp_ref.shape
        me = me_ref[0]
        owners = cnt_ref.shape[0]
        examples = len_ref.shape[0]
        first = lax.fori_loop(0, owners, lambda k, c: c + jnp.where(k < me, cnt_ref[k], 0), jnp.int32(0))
        mine = cnt_ref[me]
        gp = lax.dot_general(all_ref[...], pout_ref[...], NT, preferred_element_type=F32)
        gp = jnp.concatenate([gp, gp], axis=1)
        t = lax.broadcasted_iota(jnp.int32, (tokens, rank), 0)
        left = lax.broadcasted_iota(jnp.int32, (1, 2 * rank), 1) < rank
        for j in range(OWN_CAP):
            e = first + j
            begin, end = lax.fori_loop(
                0, examples,
                lambda k, c: (c[0] + jnp.where(k < e, len_ref[k], 0), c[1] + jnp.where(k <= e, len_ref[k], 0)),
                (jnp.int32(0), jnp.int32(0)),
            )
            end = jnp.where(j < mine, end, begin)
            hp = jnp.where((t >= begin) & (t < end), hp_ref[...], 0.0)
            s = lax.dot_general(
                hp, gp, TN, precision=lax.Precision.HIGHEST, preferred_element_type=F32
            )
            for p in range(rank // 2):
                sk_ref[j : j + 1, 2 * p * rank : 2 * (p + 1) * rank] = jnp.where(
                    left, s[2 * p : 2 * p + 1, :], s[2 * p + 1 : 2 * p + 2, :]
                )


def weight(hidden, everyone, gh, hp, pout_t, lengths, counts, me):
    tokens, rows = hidden.shape
    width = everyone.shape[1]
    rank = hp.shape[1]
    tile = 128 if rows % 128 == 0 else rows
    whole = lambda i: (0, 0)
    smem = pl.BlockSpec(memory_space=pltpu.SMEM)
    return pl.pallas_call(
        weight_kernel,
        grid=(rows // tile,),
        in_specs=[
            smem, smem, smem,
            pl.BlockSpec((tokens, tile), lambda i: (0, i)),
            pl.BlockSpec((tokens, width), whole),
            pl.BlockSpec((tokens, rows), whole),
            pl.BlockSpec((tokens, rank), whole),
            pl.BlockSpec((rank, width), whole),
        ],
        out_specs=(
            pl.BlockSpec((tile, width), lambda i: (i, 0)),
            pl.BlockSpec((tokens, rows), whole),
            pl.BlockSpec((OWN_CAP, rank * rank), whole),
        ),
        out_shape=(
            jax.ShapeDtypeStruct((rows, width), BF16),
            jax.ShapeDtypeStruct((tokens, rows), BF16),
            jax.ShapeDtypeStruct((OWN_CAP, rank * rank), F32),
        ),
        compiler_params=pltpu.CompilerParams(vmem_limit_bytes=58 * 2**20),
        name="grad_weight_and_sketches",
    )(lengths, counts, me, hidden, everyone, gh, hp, pout_t)


def solution(mesh):
    tensor = mesh.shape["tensor"]

    def shards(grad_out, hidden, down_weight, proj_in, proj_out, example_lengths, owner_counts):
        everyone, gh, hp = gather(tensor, grad_out, hidden, proj_in.T, down_weight)
        me = lax.axis_index("tensor").astype(jnp.int32).reshape(1)
        return weight(hidden, everyone, gh, hp, proj_out.T, example_lengths, owner_counts, me)

    return jax.shard_map(
        shards,
        mesh=mesh,
        in_specs=(
            P(("groups", "tensor"), None),
            P("groups", "tensor"),
            P("tensor", None),
            P("tensor", None),
            P(),
            P("groups"),
            P("groups"),
        ),
        out_specs=(
            P(("groups", "tensor"), None),
            P("groups", "tensor"),
            P(("groups", "tensor"), None),
        ),
        check_vma=False,
    )
```

```python
import functools
import jax
import jax.numpy as jnp
from jax import lax
from jax.experimental import pallas as pl
from jax.experimental.pallas import tpu as pltpu
from jax.sharding import PartitionSpec as P

OWN_CAP = 3
SLOW = 4
CUTS = 4
HALVES = 2
NT = (((1,), (1,)), ((), ()))
TN = (((0,), (0,)), ((), ()))
F32 = jnp.float32
BF16 = jnp.bfloat16


def row_tile(width):
    return 256 if width % 256 == 0 else width


def gather_kernel(
    fast, g_ref, hid_ref, pin_ref, w_ref, pout_ref, all_ref, gh_ref, hp_ref, gp_ref,
    buf, wide, wbuf, pbuf, acc, part, stage_a, stage_b, stage_c, wsem, psem,
    s1s, s1r, s2s, s2r, s3s, s3r, pas, par, pbs, pbr, pcs, pcr,
):
    me = lax.axis_index("tensor")
    core = lax.rem(me, 2)
    chip = lax.div(me, 2)
    b = lax.rem(chip, fast)
    a = lax.div(chip, fast)
    cut = buf.shape[-1]
    per = buf.shape[-2]

    def w_copy(c):
        columns = pl.ds(c * cut, cut)
        return pltpu.make_async_copy(w_ref.at[:, columns], wbuf.at[:, columns], wsem.at[c])

    p_copy = pltpu.make_async_copy(pout_ref, pbuf, psem.at[0])
    for c in range(CUTS):
        w_copy(c).start()
        if c == 0:
            p_copy.start()

    def index(ai, bi, ci):
        return (ai * fast + bi) * 2 + ci

    def up(value, step, size):
        return lax.rem(value + step, size)

    def down(value, step, size):
        return lax.rem(value + size - step, size)

    barrier = pltpu.get_barrier_semaphore()
    peers = [index(up(a, s, SLOW), b, core) for s in range(1, SLOW)]
    peers += [index(a, up(b, r, fast), core) for r in range(1, fast)]
    sibling = index(a, b, 1 - core)
    peers += [sibling]
    for peer in peers:
        pl.semaphore_signal(barrier, inc=1, device_id={"tensor": peer}, device_id_type=pl.DeviceIdType.MESH)
    for c in range(CUTS):
        buf[c, core, b, a] = g_ref[:, c * cut : (c + 1) * cut]
    part[0] = lax.dot_general(hid_ref[...], pin_ref[...], NT, preferred_element_type=F32)
    pl.semaphore_wait(barrier, len(peers))

    def send(src, dst, ssem, rsem, peer):
        return pltpu.make_async_remote_copy(
            src_ref=src, dst_ref=dst, send_sem=ssem, recv_sem=rsem,
            device_id={"tensor": peer}, device_id_type=pl.DeviceIdType.MESH,
        )

    sends = []

    def go(src, dst, ssem, rsem, peer):
        copy = send(src, dst, ssem, rsem, peer)
        copy.start()
        sends.append(copy)

    def landed(dst, sem):
        send(dst, dst, sem, sem, sibling).wait_recv()

    def first(c):
        block = buf.at[c, core, b, a]
        for s in (2, 1, 3):
            go(block, block, s1s.at[c, s], s1r.at[c, s], index(up(a, s, SLOW), b, core))

    def second(c):
        for s in range(1, SLOW):
            landed(buf.at[c, core, b, down(a, s, SLOW)], s1r.at[c, s])
        block = buf.at[c, core, b]
        for r in range(1, fast):
            go(block, block, s2s.at[c, r], s2r.at[c, r], index(a, up(b, r, fast), core))

    def third(c):
        for r in range(1, fast):
            landed(buf.at[c, core, down(b, r, fast)], s2r.at[c, r])
        block = buf.at[c, core]
        go(block, block, s3s.at[c], s3r.at[c], sibling)

    def multiply(c):
        landed(buf.at[c, 1 - core], s3r.at[c])
        for ai in range(SLOW):
            for bi in range(fast):
                for ci in range(2):
                    row = index(ai, bi, ci) * per
                    wide[row : row + per, :] = buf[c, ci, bi, ai].astype(F32)
        columns = slice(c * cut, (c + 1) * cut)
        all_ref[:, columns] = wide[...].astype(BF16)
        if c == 0:
            p_copy.wait()
        w_copy(c).wait()
        here = all_ref[:, columns]
        term = lax.dot_general(here, wbuf[:, columns], NT, preferred_element_type=F32)
        own = lax.dot_general(here, pbuf[:, columns], NT, preferred_element_type=F32)
        if c == 0:
            acc[...] = term
            gp_ref[...] = own
        elif c < CUTS - 1:
            acc[...] += term
            gp_ref[...] += own
        else:
            gh_ref[...] = (acc[...] + term).astype(BF16)
            gp_ref[...] += own

    first(0)
    for s in range(1, SLOW):
        go(part.at[0], stage_a.at[s], pas.at[s], par.at[s], index(up(a, s, SLOW), b, core))
    for c in range(1, CUTS):
        first(c)
    second(0)
    second(1)
    third(0)
    total = part[0]
    for s in range(1, SLOW):
        landed(stage_a.at[s], par.at[s])
        total = total + stage_a[s]
    part[1] = total
    for r in range(1, fast):
        go(part.at[1], stage_b.at[r], pbs.at[r], pbr.at[r], index(a, up(b, r, fast), core))
    for c in range(CUTS):
        if c + 2 < CUTS:
            second(c + 2)
        if c + 1 < CUTS:
            third(c + 1)
        if c == 1:
            for r in range(1, fast):
                landed(stage_b.at[r], pbr.at[r])
                total = total + stage_b[r]
            part[2] = total
            go(part.at[2], stage_c.at[0], pcs.at[0], pcr.at[0], sibling)
        multiply(c)

    landed(stage_c.at[0], pcr.at[0])
    hp_ref[...] = part[2] + stage_c[0]
    for copy in sends:
        copy.wait_send()


def gather(tensor, g, hidden, pin_t, w, pout_t):
    per, width = g.shape
    tokens, rows = hidden.shape
    rank = pin_t.shape[0]
    fast = tensor // (2 * SLOW)
    cut = width // CUTS
    dma = pltpu.SemaphoreType.DMA
    vmem = pl.BlockSpec(memory_space=pltpu.VMEM)
    hbm = pl.BlockSpec(memory_space=pl.ANY)
    return pl.pallas_call(
        functools.partial(gather_kernel, fast),
        out_shape=(
            jax.ShapeDtypeStruct((tokens, width), BF16),
            jax.ShapeDtypeStruct((tokens, rows), BF16),
            jax.ShapeDtypeStruct((tokens, rank), F32),
            jax.ShapeDtypeStruct((tokens, rank), F32),
        ),
        in_specs=[vmem, vmem, vmem, hbm, hbm],
        out_specs=(vmem, vmem, vmem, vmem),
        scratch_shapes=[
            pltpu.VMEM((CUTS, 2, fast, SLOW, per, cut), BF16),
            pltpu.VMEM((tokens, cut), F32),
            pltpu.VMEM((rows, width), BF16),
            pltpu.VMEM((rank, width), BF16),
            pltpu.VMEM((tokens, rows), F32),
            pltpu.VMEM((3, tokens, rank), F32),
            pltpu.VMEM((SLOW, tokens, rank), F32),
            pltpu.VMEM((fast, tokens, rank), F32),
            pltpu.VMEM((1, tokens, rank), F32),
            dma((CUTS,)), dma((1,)),
            dma((CUTS, SLOW)), dma((CUTS, SLOW)),
            dma((CUTS, fast)), dma((CUTS, fast)),
            dma((CUTS,)), dma((CUTS,)),
            dma((SLOW,)), dma((SLOW,)),
            dma((fast,)), dma((fast,)),
            dma((1,)), dma((1,)),
        ],
        compiler_params=pltpu.CompilerParams(
            collective_id=0, has_side_effects=True, vmem_limit_bytes=58 * 2**20
        ),
        name="gather_and_grad_hidden",
    )(g, hidden, pin_t, w, pout_t)


def weight_kernel(
    len_ref, cnt_ref, me_ref, hid_ref, all_ref, gh_in, hp_ref, gp_ref,
    gw_ref, gh_ref, sk_ref, obuf, osem,
):
    rows, width = obuf.shape
    tile = row_tile(rows)
    half = width // HALVES
    copies = []
    for i in range(rows // tile):
        for h in range(HALVES):
            at = (pl.ds(i * tile, tile), pl.ds(h * half, half))
            obuf[i * tile : (i + 1) * tile, h * half : (h + 1) * half] = lax.dot_general(
                hid_ref[:, i * tile : (i + 1) * tile], all_ref[:, h * half : (h + 1) * half],
                TN, preferred_element_type=F32,
            ).astype(BF16)
            copy = pltpu.make_async_copy(obuf.at[at], gw_ref.at[at], osem.at[i, h])
            copy.start()
            copies.append(copy)

    gh_ref[...] = gh_in[...]
    tokens, rank = hp_ref.shape
    me = me_ref[0]
    owners = cnt_ref.shape[0]
    examples = len_ref.shape[0]
    first = lax.fori_loop(0, owners, lambda k, c: c + jnp.where(k < me, cnt_ref[k], 0), jnp.int32(0))
    mine = cnt_ref[me]
    gp = jnp.concatenate([gp_ref[...], gp_ref[...]], axis=1)
    t = lax.broadcasted_iota(jnp.int32, (tokens, rank), 0)
    left = lax.broadcasted_iota(jnp.int32, (1, 2 * rank), 1) < rank
    for j in range(OWN_CAP):
        e = first + j
        begin, end = lax.fori_loop(
            0, examples,
            lambda k, c: (c[0] + jnp.where(k < e, len_ref[k], 0), c[1] + jnp.where(k <= e, len_ref[k], 0)),
            (jnp.int32(0), jnp.int32(0)),
        )
        end = jnp.where(j < mine, end, begin)
        hp = jnp.where((t >= begin) & (t < end), hp_ref[...], 0.0)
        s = lax.dot_general(hp, gp, TN, precision=lax.Precision.HIGHEST, preferred_element_type=F32)
        for p in range(rank // 2):
            sk_ref[j : j + 1, 2 * p * rank : 2 * (p + 1) * rank] = jnp.where(
                left, s[2 * p : 2 * p + 1, :], s[2 * p + 1 : 2 * p + 2, :]
            )
    for copy in copies:
        copy.wait()


def weight(hidden, everyone, gh, hp, gp, lengths, counts, me):
    tokens, rows = hidden.shape
    width = everyone.shape[1]
    rank = hp.shape[1]
    smem = pl.BlockSpec(memory_space=pltpu.SMEM)
    vmem = pl.BlockSpec(memory_space=pltpu.VMEM)
    return pl.pallas_call(
        weight_kernel,
        in_specs=[smem] * 3 + [vmem] * 5,
        out_specs=(pl.BlockSpec(memory_space=pl.ANY), vmem, vmem),
        out_shape=(
            jax.ShapeDtypeStruct((rows, width), BF16),
            jax.ShapeDtypeStruct((tokens, rows), BF16),
            jax.ShapeDtypeStruct((OWN_CAP, rank * rank), F32),
        ),
        scratch_shapes=[
            pltpu.VMEM((rows, width), BF16),
            pltpu.SemaphoreType.DMA((rows // row_tile(rows), HALVES)),
        ],
        compiler_params=pltpu.CompilerParams(vmem_limit_bytes=58 * 2**20),
        name="grad_weight_and_sketches",
    )(lengths, counts, me, hidden, everyone, gh, hp, gp)


def solution(mesh):
    tensor = mesh.shape["tensor"]

    def shards(grad_out, hidden, down_weight, proj_in, proj_out, example_lengths, owner_counts):
        everyone, gh, hp, gp = gather(tensor, grad_out, hidden, proj_in.T, down_weight, proj_out.T)
        me = lax.axis_index("tensor").astype(jnp.int32).reshape(1)
        return weight(hidden, everyone, gh, hp, gp, example_lengths, owner_counts, me)

    return jax.shard_map(
        shards,
        mesh=mesh,
        in_specs=(
            P(("groups", "tensor"), None),
            P("groups", "tensor"),
            P("tensor", None),
            P("tensor", None),
            P(),
            P("groups"),
            P("groups"),
        ),
        out_specs=(
            P(("groups", "tensor"), None),
            P("groups", "tensor"),
            P(("groups", "tensor"), None),
        ),
        check_vma=False,
    )
```

```python
import functools
import jax
import jax.numpy as jnp
from jax import lax
from jax.experimental import pallas as pl
from jax.experimental.pallas import tpu as pltpu
from jax.sharding import PartitionSpec as P

OWN_CAP = 3
SLOW = 4
CUTS = 4
HALVES = 2
FOLD = 16
LANE = 128
NT = (((1,), (1,)), ((), ()))
TN = (((0,), (0,)), ((), ()))
F32 = jnp.float32
BF16 = jnp.bfloat16


def row_tile(width):
    return 256 if width % 256 == 0 else width


def gather_kernel(
    fast, g_ref, hid_ref, pin_ref, w_ref, pout_ref, all_ref, gh_ref, hp_ref, gp_ref,
    buf, flat, packed, wbuf, pbuf, acc, part, stage_a, stage_b, stage_c, wsem, psem,
    s1s, s1r, s2s, s2r, s3s, s3r, pas, par, pbs, pbr, pcs, pcr,
):
    me = lax.axis_index("tensor")
    core = lax.rem(me, 2)
    chip = lax.div(me, 2)
    b = lax.rem(chip, fast)
    a = lax.div(chip, fast)
    per = g_ref.shape[0]
    cut = g_ref.shape[1] // CUTS
    tokens = hid_ref.shape[0]
    folds = FOLD // per
    lanes = cut // (folds * LANE)
    columns_of = cut // LANE

    def w_copy(c):
        columns = pl.ds(c * cut, cut)
        return pltpu.make_async_copy(w_ref.at[:, columns], wbuf.at[:, columns], wsem.at[c])

    p_copy = pltpu.make_async_copy(pout_ref, pbuf, psem.at[0])
    for c in range(CUTS):
        w_copy(c).start()
        if c == 0:
            p_copy.start()

    def index(ai, bi, ci):
        return (ai * fast + bi) * 2 + ci

    def up(value, step, size):
        return lax.rem(value + step, size)

    def down(value, step, size):
        return lax.rem(value + size - step, size)

    barrier = pltpu.get_barrier_semaphore()
    peers = [index(up(a, s, SLOW), b, core) for s in range(1, SLOW)]
    peers += [index(a, up(b, r, fast), core) for r in range(1, fast)]
    sibling = index(a, b, 1 - core)
    peers += [sibling]
    for peer in peers:
        pl.semaphore_signal(barrier, inc=1, device_id={"tensor": peer}, device_id_type=pl.DeviceIdType.MESH)
    for c in range(CUTS):
        mine = g_ref[:, c * cut : (c + 1) * cut].astype(F32)
        for t in range(per):
            for j in range(folds):
                packed[t * folds + j : t * folds + j + 1, :] = mine[
                    t : t + 1, j * lanes * LANE : (j + 1) * lanes * LANE
                ]
        buf[c, core, b, a] = packed[...].astype(BF16)
    part[0] = lax.dot_general(hid_ref[...], pin_ref[...], NT, preferred_element_type=F32)
    pl.semaphore_wait(barrier, len(peers))

    def send(src, dst, ssem, rsem, peer):
        return pltpu.make_async_remote_copy(
            src_ref=src, dst_ref=dst, send_sem=ssem, recv_sem=rsem,
            device_id={"tensor": peer}, device_id_type=pl.DeviceIdType.MESH,
        )

    sends = []

    def go(src, dst, ssem, rsem, peer):
        copy = send(src, dst, ssem, rsem, peer)
        copy.start()
        sends.append(copy)

    def landed(dst, sem):
        send(dst, dst, sem, sem, sibling).wait_recv()

    def first(c):
        block = buf.at[c, core, b, a]
        for s in (2, 1, 3):
            go(block, block, s1s.at[c, s], s1r.at[c, s], index(up(a, s, SLOW), b, core))

    def second(c):
        for s in range(1, SLOW):
            landed(buf.at[c, core, b, down(a, s, SLOW)], s1r.at[c, s])
        block = buf.at[c, core, b]
        for r in range(1, fast):
            go(block, block, s2s.at[c, r], s2r.at[c, r], index(a, up(b, r, fast), core))

    def third(c):
        for r in range(1, fast):
            landed(buf.at[c, core, down(b, r, fast)], s2r.at[c, r])
        block = buf.at[c, core]
        go(block, block, s3s.at[c], s3r.at[c], sibling)

    def multiply(c):
        landed(buf.at[c, 1 - core], s3r.at[c])
        for ai in range(SLOW):
            for bi in range(fast):
                for ci in range(2):
                    block = buf[c, ci, bi, ai].astype(F32)
                    for t in range(per):
                        group, row = divmod(index(ai, bi, ci) * per + t, 8)
                        for l in range(lanes):
                            flat[pl.ds((group * columns_of + l) * 8 + row, folds, stride=lanes * 8), :] = block[
                                t * folds : (t + 1) * folds, l * LANE : (l + 1) * LANE
                            ]
        for k in range(columns_of):
            for q in range(tokens // 16):
                top = (2 * q * columns_of + k) * 8
                low = ((2 * q + 1) * columns_of + k) * 8
                all_ref[q * 16 : (q + 1) * 16, c * cut + k * LANE : c * cut + (k + 1) * LANE] = jnp.concatenate(
                    [flat[top : top + 8, :], flat[low : low + 8, :]], axis=0
                ).astype(BF16)
        columns = slice(c * cut, (c + 1) * cut)
        if c == 0:
            p_copy.wait()
        w_copy(c).wait()
        here = all_ref[:, columns]
        term = lax.dot_general(here, wbuf[:, columns], NT, preferred_element_type=F32)
        own = lax.dot_general(here, pbuf[:, columns], NT, preferred_element_type=F32)
        if c == 0:
            acc[...] = term
            gp_ref[...] = own
        elif c < CUTS - 1:
            acc[...] += term
            gp_ref[...] += own
        else:
            gh_ref[...] = (acc[...] + term).astype(BF16)
            gp_ref[...] += own

    first(0)
    for s in range(1, SLOW):
        go(part.at[0], stage_a.at[s], pas.at[s], par.at[s], index(up(a, s, SLOW), b, core))
    for c in range(1, CUTS):
        first(c)
    second(0)
    second(1)
    third(0)
    total = part[0]
    for s in range(1, SLOW):
        landed(stage_a.at[s], par.at[s])
        total = total + stage_a[s]
    part[1] = total
    for r in range(1, fast):
        go(part.at[1], stage_b.at[r], pbs.at[r], pbr.at[r], index(a, up(b, r, fast), core))
    for c in range(CUTS):
        if c + 2 < CUTS:
            second(c + 2)
        if c + 1 < CUTS:
            third(c + 1)
        if c == 1:
            for r in range(1, fast):
                landed(stage_b.at[r], pbr.at[r])
                total = total + stage_b[r]
            part[2] = total
            go(part.at[2], stage_c.at[0], pcs.at[0], pcr.at[0], sibling)
        multiply(c)

    landed(stage_c.at[0], pcr.at[0])
    hp_ref[...] = part[2] + stage_c[0]
    for copy in sends:
        copy.wait_send()


def gather(tensor, g, hidden, pin_t, w, pout_t):
    per, width = g.shape
    tokens, rows = hidden.shape
    rank = pin_t.shape[0]
    fast = tensor // (2 * SLOW)
    cut = width // CUTS
    dma = pltpu.SemaphoreType.DMA
    vmem = pl.BlockSpec(memory_space=pltpu.VMEM)
    hbm = pl.BlockSpec(memory_space=pl.ANY)
    return pl.pallas_call(
        functools.partial(gather_kernel, fast),
        out_shape=(
            jax.ShapeDtypeStruct((tokens, width), BF16),
            jax.ShapeDtypeStruct((tokens, rows), BF16),
            jax.ShapeDtypeStruct((tokens, rank), F32),
            jax.ShapeDtypeStruct((tokens, rank), F32),
        ),
        in_specs=[vmem, vmem, vmem, hbm, hbm],
        out_specs=(vmem, vmem, vmem, vmem),
        scratch_shapes=[
            pltpu.VMEM((CUTS, 2, fast, SLOW, FOLD, per * cut // FOLD), BF16),
            pltpu.VMEM((tokens * cut // LANE, LANE), F32),
            pltpu.VMEM((FOLD, per * cut // FOLD), F32),
            pltpu.VMEM((rows, width), BF16),
            pltpu.VMEM((rank, width), BF16),
            pltpu.VMEM((tokens, rows), F32),
            pltpu.VMEM((3, tokens, rank), F32),
            pltpu.VMEM((SLOW, tokens, rank), F32),
            pltpu.VMEM((fast, tokens, rank), F32),
            pltpu.VMEM((1, tokens, rank), F32),
            dma((CUTS,)), dma((1,)),
            dma((CUTS, SLOW)), dma((CUTS, SLOW)),
            dma((CUTS, fast)), dma((CUTS, fast)),
            dma((CUTS,)), dma((CUTS,)),
            dma((SLOW,)), dma((SLOW,)),
            dma((fast,)), dma((fast,)),
            dma((1,)), dma((1,)),
        ],
        compiler_params=pltpu.CompilerParams(
            collective_id=0, has_side_effects=True, vmem_limit_bytes=58 * 2**20
        ),
        name="gather_and_grad_hidden",
    )(g, hidden, pin_t, w, pout_t)


def weight_kernel(
    len_ref, cnt_ref, me_ref, hid_ref, all_ref, gh_in, hp_ref, gp_ref,
    gw_ref, gh_ref, sk_ref, obuf, osem,
):
    rows, width = obuf.shape
    tile = row_tile(rows)
    half = width // HALVES
    copies = []
    for i in range(rows // tile):
        for h in range(HALVES):
            at = (pl.ds(i * tile, tile), pl.ds(h * half, half))
            obuf[i * tile : (i + 1) * tile, h * half : (h + 1) * half] = lax.dot_general(
                hid_ref[:, i * tile : (i + 1) * tile], all_ref[:, h * half : (h + 1) * half],
                TN, preferred_element_type=F32,
            ).astype(BF16)
            copy = pltpu.make_async_copy(obuf.at[at], gw_ref.at[at], osem.at[i, h])
            copy.start()
            copies.append(copy)

    gh_ref[...] = gh_in[...]
    tokens, rank = hp_ref.shape
    me = me_ref[0]
    owners = cnt_ref.shape[0]
    examples = len_ref.shape[0]
    first = lax.fori_loop(0, owners, lambda k, c: c + jnp.where(k < me, cnt_ref[k], 0), jnp.int32(0))
    mine = cnt_ref[me]
    gp = jnp.concatenate([gp_ref[...], gp_ref[...]], axis=1)
    t = lax.broadcasted_iota(jnp.int32, (tokens, rank), 0)
    left = lax.broadcasted_iota(jnp.int32, (1, 2 * rank), 1) < rank
    for j in range(OWN_CAP):
        e = first + j
        begin, end = lax.fori_loop(
            0, examples,
            lambda k, c: (c[0] + jnp.where(k < e, len_ref[k], 0), c[1] + jnp.where(k <= e, len_ref[k], 0)),
            (jnp.int32(0), jnp.int32(0)),
        )
        end = jnp.where(j < mine, end, begin)
        hp = jnp.where((t >= begin) & (t < end), hp_ref[...], 0.0)
        s = lax.dot_general(hp, gp, TN, precision=lax.Precision.HIGHEST, preferred_element_type=F32)
        for p in range(rank // 2):
            sk_ref[j : j + 1, 2 * p * rank : 2 * (p + 1) * rank] = jnp.where(
                left, s[2 * p : 2 * p + 1, :], s[2 * p + 1 : 2 * p + 2, :]
            )
    for copy in copies:
        copy.wait()


def weight(hidden, everyone, gh, hp, gp, lengths, counts, me):
    tokens, rows = hidden.shape
    width = everyone.shape[1]
    rank = hp.shape[1]
    smem = pl.BlockSpec(memory_space=pltpu.SMEM)
    vmem = pl.BlockSpec(memory_space=pltpu.VMEM)
    return pl.pallas_call(
        weight_kernel,
        in_specs=[smem] * 3 + [vmem] * 5,
        out_specs=(pl.BlockSpec(memory_space=pl.ANY), vmem, vmem),
        out_shape=(
            jax.ShapeDtypeStruct((rows, width), BF16),
            jax.ShapeDtypeStruct((tokens, rows), BF16),
            jax.ShapeDtypeStruct((OWN_CAP, rank * rank), F32),
        ),
        scratch_shapes=[
            pltpu.VMEM((rows, width), BF16),
            pltpu.SemaphoreType.DMA((rows // row_tile(rows), HALVES)),
        ],
        compiler_params=pltpu.CompilerParams(vmem_limit_bytes=58 * 2**20),
        name="grad_weight_and_sketches",
    )(lengths, counts, me, hidden, everyone, gh, hp, gp)


def solution(mesh):
    tensor = mesh.shape["tensor"]

    def shards(grad_out, hidden, down_weight, proj_in, proj_out, example_lengths, owner_counts):
        everyone, gh, hp, gp = gather(tensor, grad_out, hidden, proj_in.T, down_weight, proj_out.T)
        me = lax.axis_index("tensor").astype(jnp.int32).reshape(1)
        return weight(hidden, everyone, gh, hp, gp, example_lengths, owner_counts, me)

    return jax.shard_map(
        shards,
        mesh=mesh,
        in_specs=(
            P(("groups", "tensor"), None),
            P("groups", "tensor"),
            P("tensor", None),
            P("tensor", None),
            P(),
            P("groups"),
            P("groups"),
        ),
        out_specs=(
            P(("groups", "tensor"), None),
            P("groups", "tensor"),
            P(("groups", "tensor"), None),
        ),
        check_vma=False,
    )
```

```python
import functools
import jax
import jax.numpy as jnp
from jax import lax
from jax.experimental import pallas as pl
from jax.experimental.pallas import tpu as pltpu
from jax.sharding import PartitionSpec as P

OWN_CAP = 3
SLOW = 4
CUTS = 4
HALVES = 2
NT = (((1,), (1,)), ((), ()))
TN = (((0,), (0,)), ((), ()))
F32 = jnp.float32
BF16 = jnp.bfloat16


def row_tile(width):
    return 256 if width % 256 == 0 else width


def gather_kernel(
    fast, g_ref, hid_ref, pin_ref, w_ref, pout_ref, all_ref, gh_ref, hp_ref, gp_ref,
    buf, wide, wbuf, pbuf, acc, part, stage_a, stage_b, stage_c, wsem, psem,
    s1s, s1r, s2s, s2r, s3s, s3r, pas, par, pbs, pbr, pcs, pcr,
):
    me = lax.axis_index("tensor")
    core = lax.rem(me, 2)
    chip = lax.div(me, 2)
    b = lax.rem(chip, fast)
    a = lax.div(chip, fast)
    cut = buf.shape[-1]
    per = buf.shape[-2]

    def w_copy(c):
        columns = pl.ds(c * cut, cut)
        return pltpu.make_async_copy(w_ref.at[:, columns], wbuf.at[:, columns], wsem.at[c])

    p_copy = pltpu.make_async_copy(pout_ref, pbuf, psem.at[0])
    for c in range(CUTS):
        w_copy(c).start()
        if c == 0:
            p_copy.start()

    def index(ai, bi, ci):
        return (ai * fast + bi) * 2 + ci

    def up(value, step, size):
        return lax.rem(value + step, size)

    def down(value, step, size):
        return lax.rem(value + size - step, size)

    barrier = pltpu.get_barrier_semaphore()
    peers = [index(up(a, s, SLOW), b, core) for s in range(1, SLOW)]
    peers += [index(a, up(b, r, fast), core) for r in range(1, fast)]
    sibling = index(a, b, 1 - core)
    peers += [sibling]
    for peer in peers:
        pl.semaphore_signal(barrier, inc=1, device_id={"tensor": peer}, device_id_type=pl.DeviceIdType.MESH)
    for c in range(CUTS):
        buf[c, core, b, a] = g_ref[:, c * cut : (c + 1) * cut]
    part[0] = lax.dot_general(hid_ref[...], pin_ref[...], NT, preferred_element_type=F32)
    pl.semaphore_wait(barrier, len(peers))

    def send(src, dst, ssem, rsem, peer):
        return pltpu.make_async_remote_copy(
            src_ref=src, dst_ref=dst, send_sem=ssem, recv_sem=rsem,
            device_id={"tensor": peer}, device_id_type=pl.DeviceIdType.MESH,
        )

    sends = []

    def go(src, dst, ssem, rsem, peer):
        copy = send(src, dst, ssem, rsem, peer)
        copy.start()
        sends.append(copy)

    def landed(dst, sem):
        send(dst, dst, sem, sem, sibling).wait_recv()

    def first(c):
        block = buf.at[c, core, b, a]
        for s in (2, 1, 3):
            go(block, block, s1s.at[c, s], s1r.at[c, s], index(up(a, s, SLOW), b, core))

    def second(c):
        for s in range(1, SLOW):
            landed(buf.at[c, core, b, down(a, s, SLOW)], s1r.at[c, s])
        block = buf.at[c, core, b]
        for r in range(1, fast):
            go(block, block, s2s.at[c, r], s2r.at[c, r], index(a, up(b, r, fast), core))
        go(block, block, s3s.at[c, 0], s3r.at[c, 0], sibling)

    def third(c):
        for r in range(1, fast):
            block = buf.at[c, core, down(b, r, fast)]
            landed(block, s2r.at[c, r])
            go(block, block, s3s.at[c, r], s3r.at[c, r], sibling)

    def multiply(c):
        for r in range(fast):
            landed(buf.at[c, 1 - core, down(b, r, fast)], s3r.at[c, r])
        for ai in range(SLOW):
            for bi in range(fast):
                for ci in range(2):
                    row = index(ai, bi, ci) * per
                    wide[row : row + per, :] = buf[c, ci, bi, ai].astype(F32)
        columns = slice(c * cut, (c + 1) * cut)
        all_ref[:, columns] = wide[...].astype(BF16)
        if c == 0:
            p_copy.wait()
        w_copy(c).wait()
        here = all_ref[:, columns]
        term = lax.dot_general(here, wbuf[:, columns], NT, preferred_element_type=F32)
        own = lax.dot_general(here, pbuf[:, columns], NT, preferred_element_type=F32)
        if c == 0:
            acc[...] = term
            gp_ref[...] = own
        elif c < CUTS - 1:
            acc[...] += term
            gp_ref[...] += own
        else:
            gh_ref[...] = (acc[...] + term).astype(BF16)
            gp_ref[...] += own

    first(0)
    for s in range(1, SLOW):
        go(part.at[0], stage_a.at[s], pas.at[s], par.at[s], index(up(a, s, SLOW), b, core))
    for c in range(1, CUTS):
        first(c)
    second(0)
    second(1)
    third(0)
    total = part[0]
    for s in range(1, SLOW):
        landed(stage_a.at[s], par.at[s])
        total = total + stage_a[s]
    part[1] = total
    for r in range(1, fast):
        go(part.at[1], stage_b.at[r], pbs.at[r], pbr.at[r], index(a, up(b, r, fast), core))
    for c in range(CUTS):
        if c + 2 < CUTS:
            second(c + 2)
        if c + 1 < CUTS:
            third(c + 1)
        if c == 1:
            for r in range(1, fast):
                landed(stage_b.at[r], pbr.at[r])
                total = total + stage_b[r]
            part[2] = total
            go(part.at[2], stage_c.at[0], pcs.at[0], pcr.at[0], sibling)
        multiply(c)

    landed(stage_c.at[0], pcr.at[0])
    hp_ref[...] = part[2] + stage_c[0]
    for copy in sends:
        copy.wait_send()


def gather(tensor, g, hidden, pin_t, w, pout_t):
    per, width = g.shape
    tokens, rows = hidden.shape
    rank = pin_t.shape[0]
    fast = tensor // (2 * SLOW)
    cut = width // CUTS
    dma = pltpu.SemaphoreType.DMA
    vmem = pl.BlockSpec(memory_space=pltpu.VMEM)
    hbm = pl.BlockSpec(memory_space=pl.ANY)
    return pl.pallas_call(
        functools.partial(gather_kernel, fast),
        out_shape=(
            jax.ShapeDtypeStruct((tokens, width), BF16),
            jax.ShapeDtypeStruct((tokens, rows), BF16),
            jax.ShapeDtypeStruct((tokens, rank), F32),
            jax.ShapeDtypeStruct((tokens, rank), F32),
        ),
        in_specs=[vmem, vmem, vmem, hbm, hbm],
        out_specs=(vmem, vmem, vmem, vmem),
        scratch_shapes=[
            pltpu.VMEM((CUTS, 2, fast, SLOW, per, cut), BF16),
            pltpu.VMEM((tokens, cut), F32),
            pltpu.VMEM((rows, width), BF16),
            pltpu.VMEM((rank, width), BF16),
            pltpu.VMEM((tokens, rows), F32),
            pltpu.VMEM((3, tokens, rank), F32),
            pltpu.VMEM((SLOW, tokens, rank), F32),
            pltpu.VMEM((fast, tokens, rank), F32),
            pltpu.VMEM((1, tokens, rank), F32),
            dma((CUTS,)), dma((1,)),
            dma((CUTS, SLOW)), dma((CUTS, SLOW)),
            dma((CUTS, fast)), dma((CUTS, fast)),
            dma((CUTS, fast)), dma((CUTS, fast)),
            dma((SLOW,)), dma((SLOW,)),
            dma((fast,)), dma((fast,)),
            dma((1,)), dma((1,)),
        ],
        compiler_params=pltpu.CompilerParams(
            collective_id=0, has_side_effects=True, vmem_limit_bytes=58 * 2**20
        ),
        name="gather_and_grad_hidden",
    )(g, hidden, pin_t, w, pout_t)


def weight_kernel(
    len_ref, cnt_ref, me_ref, hid_ref, all_ref, gh_in, hp_ref, gp_ref,
    gw_ref, gh_ref, sk_ref, obuf, osem,
):
    rows, width = obuf.shape
    tile = row_tile(rows)
    half = width // HALVES
    copies = []
    for i in range(rows // tile):
        for h in range(HALVES):
            at = (pl.ds(i * tile, tile), pl.ds(h * half, half))
            obuf[i * tile : (i + 1) * tile, h * half : (h + 1) * half] = lax.dot_general(
                hid_ref[:, i * tile : (i + 1) * tile], all_ref[:, h * half : (h + 1) * half],
                TN, preferred_element_type=F32,
            ).astype(BF16)
            copy = pltpu.make_async_copy(obuf.at[at], gw_ref.at[at], osem.at[i, h])
            copy.start()
            copies.append(copy)

    gh_ref[...] = gh_in[...]
    tokens, rank = hp_ref.shape
    me = me_ref[0]
    owners = cnt_ref.shape[0]
    examples = len_ref.shape[0]
    first = lax.fori_loop(0, owners, lambda k, c: c + jnp.where(k < me, cnt_ref[k], 0), jnp.int32(0))
    mine = cnt_ref[me]
    gp = jnp.concatenate([gp_ref[...], gp_ref[...]], axis=1)
    t = lax.broadcasted_iota(jnp.int32, (tokens, rank), 0)
    left = lax.broadcasted_iota(jnp.int32, (1, 2 * rank), 1) < rank
    for j in range(OWN_CAP):
        e = first + j
        begin, end = lax.fori_loop(
            0, examples,
            lambda k, c: (c[0] + jnp.where(k < e, len_ref[k], 0), c[1] + jnp.where(k <= e, len_ref[k], 0)),
            (jnp.int32(0), jnp.int32(0)),
        )
        end = jnp.where(j < mine, end, begin)
        hp = jnp.where((t >= begin) & (t < end), hp_ref[...], 0.0)
        s = lax.dot_general(hp, gp, TN, precision=lax.Precision.HIGHEST, preferred_element_type=F32)
        for p in range(rank // 2):
            sk_ref[j : j + 1, 2 * p * rank : 2 * (p + 1) * rank] = jnp.where(
                left, s[2 * p : 2 * p + 1, :], s[2 * p + 1 : 2 * p + 2, :]
            )
    for copy in copies:
        copy.wait()


def weight(hidden, everyone, gh, hp, gp, lengths, counts, me):
    tokens, rows = hidden.shape
    width = everyone.shape[1]
    rank = hp.shape[1]
    smem = pl.BlockSpec(memory_space=pltpu.SMEM)
    vmem = pl.BlockSpec(memory_space=pltpu.VMEM)
    return pl.pallas_call(
        weight_kernel,
        in_specs=[smem] * 3 + [vmem] * 5,
        out_specs=(pl.BlockSpec(memory_space=pl.ANY), vmem, vmem),
        out_shape=(
            jax.ShapeDtypeStruct((rows, width), BF16),
            jax.ShapeDtypeStruct((tokens, rows), BF16),
            jax.ShapeDtypeStruct((OWN_CAP, rank * rank), F32),
        ),
        scratch_shapes=[
            pltpu.VMEM((rows, width), BF16),
            pltpu.SemaphoreType.DMA((rows // row_tile(rows), HALVES)),
        ],
        compiler_params=pltpu.CompilerParams(vmem_limit_bytes=58 * 2**20),
        name="grad_weight_and_sketches",
    )(lengths, counts, me, hidden, everyone, gh, hp, gp)


def solution(mesh):
    tensor = mesh.shape["tensor"]

    def shards(grad_out, hidden, down_weight, proj_in, proj_out, example_lengths, owner_counts):
        everyone, gh, hp, gp = gather(tensor, grad_out, hidden, proj_in.T, down_weight, proj_out.T)
        me = lax.axis_index("tensor").astype(jnp.int32).reshape(1)
        return weight(hidden, everyone, gh, hp, gp, example_lengths, owner_counts, me)

    return jax.shard_map(
        shards,
        mesh=mesh,
        in_specs=(
            P(("groups", "tensor"), None),
            P("groups", "tensor"),
            P("tensor", None),
            P("tensor", None),
            P(),
            P("groups"),
            P("groups"),
        ),
        out_specs=(
            P(("groups", "tensor"), None),
            P("groups", "tensor"),
            P(("groups", "tensor"), None),
        ),
        check_vma=False,
    )
```
